32 devices in a mesh: rows: 4 (over y, x), sub: 8 (over z, core).
Axes of the slice: x: 2, y: 2, z: 4, core: 2. Of those that a mesh axis runs over, the one named last changes fastest.
Arguments:
- embeddings: bfloat16 [8192, 1024], P(('rows', 'sub'))
- codes: int32 [64, 8192], P(None, ('rows', 'sub')), may hold values from 0 to 255
- codebook: bfloat16 [256, 1024], P(None, 'sub'), may hold values from -6 to 6
Outputs:
- rotation: float32 [1024, 1024], P('sub')
- rotated: bfloat16 [8192, 1024], P(('rows', 'sub'))
- new_codebook: float32 [256, 1024], P(None, 'sub')
The draws below stay inside these ranges and needn't reach their ends.
All inputs are finite; a program needn't handle non-finite values.
Results may differ from the reference program's by a relative error of at most 0.0095.
Values may be sent and summed in bfloat16 or wider, within the bound.
A program may use at most 64 MiB of HBM per device.

```python
import math
import jax
import jax.numpy as jnp
import numpy as np
from jax import lax

D = 1024
SUBSPACES = 64
K = 256
SUBDIM = 16
NS_STEPS = 3
ROW_DEV = 256
ROWS = 8192


def draw_embeddings(key, part):
    key_rows, key_cols, key_base = jax.random.split(key, 3)
    row_scale = jnp.exp(jax.random.uniform(key_rows, (ROWS, 1), jnp.float32) * math.log(10.0))
    col_scale = jnp.exp(jax.random.uniform(key_cols, (1, D), jnp.float32) * math.log(10.0))
    base = jax.random.normal(key_base, (ROWS, D), jnp.float32)
    return (0.2 * row_scale * col_scale * base).astype(jnp.bfloat16)


def set_ends(array, key, low, top_value):
    shape = array.shape
    place = [jax.random.randint(jax.random.fold_in(key, axis), (), 0, shape[axis]) for axis in range(len(shape))]
    array = array.at[tuple(place)].set(low)
    longest = shape.index(max(shape))
    place[longest] = (place[longest] + 1) % shape[longest]
    return array.at[tuple(place)].set(top_value)


def block_levels(stream_key, dims, cuts, smallest, largest):
    factor_of, own = 1.0, jax.random.fold_in(stream_key, 6)
    for axis_at, blocks in cuts:
        heights = jnp.exp(jax.random.uniform(jax.random.fold_in(own, axis_at), (blocks,), jnp.float32, smallest / len(cuts), largest / len(cuts)))
        factor_of = factor_of * jnp.repeat(heights, dims[axis_at] // blocks).reshape([-1 if axis == axis_at else 1 for axis in range(len(dims))])
    return factor_of


def rank_table(count, slope):
    portions = [(1 << 20) // math.isqrt(rank ** slope) + 1 for rank in range(1, count + 1)]
    scale = 1 + sum(portions) // (1 << 30)
    return np.cumsum(np.array([max(1, weight // scale) for weight in portions]))


def ranked_ids(stream_key, dims, amount, slope):
    table = rank_table(amount, slope)
    pick = jax.random.randint(jax.random.fold_in(stream_key, 1), dims, 0, int(table[amount - 1]))
    grade = jnp.searchsorted(jnp.asarray(table, jnp.int32), pick, side="right")
    return jax.random.permutation(jax.random.fold_in(stream_key, 2), amount)[grade].astype(jnp.int32)


def noise(key, extent, scale, most, cuts=(), held_as=jnp.bfloat16):
    result = jax.random.normal(key, extent, jnp.float32) * scale
    if len(cuts) > 0:
        result = block_levels(key, extent, cuts, -0.22, 0.18) * result
    return jnp.clip(result, min=-most, max=most).astype(held_as)


def setup_inputs(seed: int = 0) -> dict:
    splits = jax.random.split(jax.random.key(seed), 4)
    embeddings = draw_embeddings(jax.random.fold_in(splits[3], 71), 0)
    codes = set_ends(ranked_ids(splits[1], (SUBSPACES, ROWS), K, 3), jax.random.fold_in(splits[1], 3), 0, K - 1).astype(jnp.int32)
    codebook = noise(splits[2], (K, D), 1.0, 6.0, ((1, 8),))
    return {"embeddings": embeddings, "codes": codes, "codebook": codebook}


coef_a = 3.4445
coef_b = -4.775
coef_c = 2.0315
frob_eps = 1e-07
highest = lax.Precision.HIGHEST

def rows_dot(left, right):
    return lax.dot_general(left, right, (((1,), (1,)), ((), ())), precision=highest, preferred_element_type=jnp.float32)

def reference(embeddings, codes, codebook):
    block_rows = ROW_DEV
    blocks = ROWS // block_rows
    codewords = codebook.astype(jnp.float32).reshape(K, SUBSPACES, SUBDIM)
    row_blocks = embeddings.reshape(blocks, block_rows, D)
    code_blocks = codes.reshape(SUBSPACES, blocks, block_rows).transpose(1, 0, 2)
    subspace_ids = lax.broadcasted_iota(jnp.int32, (SUBSPACES, block_rows), 0)

    def cross_block(running, pieces):
        picked = codewords[pieces[1], subspace_ids, :]
        decoded = picked.transpose(1, 0, 2).reshape(block_rows, D).astype(jnp.bfloat16)
        block_term = jnp.dot(pieces[0].T, decoded, preferred_element_type=jnp.float32)
        return (running + block_term, None)
    cross_cov, unused = lax.scan(cross_block, jnp.zeros((D, D), jnp.float32), (row_blocks, code_blocks))
    frob_scale = jnp.sqrt(jnp.sum(cross_cov * cross_cov)) + frob_eps
    ortho_iter = cross_cov / frob_scale
    for newton_step in range(NS_STEPS):
        gram_rows = rows_dot(ortho_iter, ortho_iter)
        quartic = rows_dot(jnp.dot(gram_rows, ortho_iter, precision=highest, preferred_element_type=jnp.float32), ortho_iter)
        mixer = coef_b * gram_rows + coef_c * quartic
        ortho_iter = coef_a * ortho_iter + jnp.dot(mixer, ortho_iter, precision=highest, preferred_element_type=jnp.float32)
    rotation = ortho_iter
    rotation_half = rotation.astype(jnp.bfloat16)

    def rotate_block(running, pieces):
        rotated_block = jnp.dot(pieces[0], rotation_half, preferred_element_type=jnp.float32).astype(jnp.bfloat16)
        segment_ids = (pieces[1] + subspace_ids * K).T.reshape(block_rows * SUBSPACES)
        values = rotated_block.astype(jnp.float32).reshape(block_rows * SUBSPACES, SUBDIM)
        block_sums = jax.ops.segment_sum(values, segment_ids, num_segments=SUBSPACES * K)
        block_counts = jax.ops.segment_sum(jnp.ones((block_rows * SUBSPACES,), jnp.float32), segment_ids, num_segments=SUBSPACES * K)
        return ((running[0] + block_sums, running[1] + block_counts), rotated_block)
    initial = (jnp.zeros((SUBSPACES * K, SUBDIM), jnp.float32), jnp.zeros((SUBSPACES * K,), jnp.float32))
    (code_sums, counts), rotated = lax.scan(rotate_block, initial, (row_blocks, code_blocks))
    rotated = rotated.reshape(ROWS, D)
    code_sums = code_sums.reshape(SUBSPACES, K, SUBDIM).transpose(1, 0, 2).reshape(K, D)
    counts = counts.reshape(SUBSPACES, K).T
    spread = jnp.repeat(counts, SUBDIM, axis=1)
    new_codebook = (code_sums + codebook.astype(jnp.float32)) / (spread + 1.0)
    return (rotation, rotated, new_codebook)
```

```python
import functools
import math

import jax
import jax.numpy as jnp
from jax import lax
from jax.experimental import pallas as pl
from jax.experimental.pallas import tpu as pltpu
from jax.sharding import PartitionSpec as P

NS_STEPS = 3


coef_a = 3.4445
coef_b = -4.775
coef_c = 2.0315
frob_eps = 1e-07
MESH = pl.DeviceIdType.MESH
VMEM_LIMIT = 56 * 1024 * 1024


def place():
    sub = lax.axis_index("sub")
    return lax.axis_index("rows"), sub // 2, sub % 2


def greet(peers):
    barrier = pltpu.get_barrier_semaphore()
    for peer in peers:
        pl.semaphore_signal(barrier, inc=1, device_id=peer, device_id_type=MESH)
    pl.semaphore_wait(barrier, len(peers))


def push(src, dst, send_sem, recv_sem, peer):
    return pltpu.make_async_remote_copy(
        src_ref=src,
        dst_ref=dst,
        send_sem=send_sem,
        recv_sem=recv_sem,
        device_id=peer,
        device_id_type=MESH,
    )


def gather_kernel(depth, block_ref, out_ref, z_send, z_recv, c_send, c_recv, local_sem):
    r, z, c = place()
    width = block_ref.shape[0]

    def slot(z_at, c_at):
        return out_ref.at[pl.ds(pl.multiple_of((z_at * 2 + c_at) * width, width), width)]

    def z_peer(step):
        return (r, lax.rem(z + step, depth) * 2 + c)

    partner = (r, z * 2 + 1 - c)
    greet([partner] + [z_peer(step) for step in range(1, depth)])
    z_copies = []
    for step in range(1, depth):
        copy = push(block_ref, slot(z, c), z_send.at[step - 1], z_recv.at[step - 1], z_peer(step))
        copy.start()
        z_copies.append(copy)
    own = pltpu.make_async_copy(block_ref, slot(z, c), local_sem)
    own.start()
    c_copies = [push(block_ref, slot(z, c), c_send.at[0], c_recv.at[0], partner)]
    c_copies[0].start()
    for step in range(1, depth):
        z_copies[step - 1].wait_recv()
        source = lax.rem(z - step + depth, depth)
        copy = push(slot(source, c), slot(source, c), c_send.at[step], c_recv.at[step], partner)
        copy.start()
        c_copies.append(copy)
    for copy in c_copies:
        copy.wait()
    for copy in z_copies:
        copy.wait_send()
    own.wait()


def gather_columns(block, subs):
    width, codewords = block.shape
    depth = subs // 2
    return pl.pallas_call(
        functools.partial(gather_kernel, depth),
        out_shape=jax.ShapeDtypeStruct((width * subs, codewords), block.dtype),
        in_specs=[pl.BlockSpec(memory_space=pltpu.VMEM)],
        out_specs=pl.BlockSpec(memory_space=pltpu.VMEM),
        scratch_shapes=[
            pltpu.SemaphoreType.DMA((max(depth - 1, 1),)),
            pltpu.SemaphoreType.DMA((max(depth - 1, 1),)),
            pltpu.SemaphoreType.DMA((depth,)),
            pltpu.SemaphoreType.DMA((depth,)),
            pltpu.SemaphoreType.DMA,
        ],
        compiler_params=pltpu.CompilerParams(
            collective_id=0, has_side_effects=True, vmem_limit_bytes=VMEM_LIMIT
        ),
        name="gather_columns",
    )(block)


def total_kernel(
    groups, depth, part_ref, out_ref, core_in, row_out, row_in, z_out, z_in,
    c_send, c_recv, r_send, r_recv, z_send, z_recv,
    gz_send, gz_recv, gr_send, gr_recv, gc_send, gc_recv,
):
    r, z, c = place()
    size, width = part_ref.shape
    half = size // 2
    rows = half // groups
    cols = width // depth
    partner = (r, z * 2 + 1 - c)

    def r_peer(step):
        return (lax.rem(r + step, groups), z * 2 + c)

    def z_peer(step):
        return (r, lax.rem(z + step, depth) * 2 + c)

    def chunk(core_at, row_at):
        return pl.ds(pl.multiple_of(core_at * half + row_at * rows, rows), rows)

    def band(z_at):
        return pl.ds(pl.multiple_of(z_at * cols, cols), cols)

    greet(
        [partner]
        + [r_peer(step) for step in range(1, groups)]
        + [z_peer(step) for step in range(1, depth)]
    )
    order = list(range(1, groups)) + [0]
    c_copies = []
    for at, step in enumerate(order):
        q = lax.rem(r + step, groups)
        copy = push(part_ref.at[chunk(1 - c, q)], core_in.at[at], c_send.at[at], c_recv.at[at], partner)
        copy.start()
        c_copies.append(copy)
    r_copies = []
    for at, step in enumerate(order):
        q = lax.rem(r + step, groups)
        c_copies[at].wait_recv()
        row_out[at] = part_ref[chunk(c, q)] + core_in[at]
        if step > 0:
            copy = push(row_out.at[at], row_in.at[at], r_send.at[at], r_recv.at[at], r_peer(step))
            copy.start()
            r_copies.append(copy)
    for copy in r_copies:
        copy.wait_recv()

    def row_sum(z_at):
        total = row_out[groups - 1, :, band(z_at)]
        for at in range(groups - 1):
            total = total + row_in[at, :, band(z_at)]
        return total

    z_copies = []
    for step in range(1, depth):
        z_out[step - 1] = row_sum(lax.rem(z + step, depth))
        copy = push(z_out.at[step - 1], z_in.at[step - 1], z_send.at[step - 1], z_recv.at[step - 1], z_peer(step))
        copy.start()
        z_copies.append(copy)
    total = row_sum(z)
    for step in range(1, depth):
        z_copies[step - 1].wait_recv()
        total = total + z_in[step - 1]
    own = (chunk(c, r), band(z))
    out_ref[own] = total

    gz_copies = []
    for step in range(1, depth):
        copy = push(out_ref.at[own], out_ref.at[own], gz_send.at[step - 1], gz_recv.at[step - 1], z_peer(step))
        copy.start()
        gz_copies.append(copy)
    gr_copies = []
    for at in range(depth):
        source = lax.rem(z - at + depth, depth)
        if at > 0:
            gz_copies[at - 1].wait_recv()
        block = (chunk(c, r), band(source))
        for step in range(1, groups):
            copy = push(out_ref.at[block], out_ref.at[block], gr_send.at[at, step - 1], gr_recv.at[at, step - 1], r_peer(step))
            copy.start()
            gr_copies.append(copy)
    gc_copies = []
    for step in range(groups):
        q = lax.rem(r - step + groups, groups)
        if step > 0:
            for at in range(depth):
                gr_copies[at * (groups - 1) + step - 1].wait_recv()
        copy = push(out_ref.at[chunk(c, q)], out_ref.at[chunk(c, q)], gc_send.at[step], gc_recv.at[step], partner)
        copy.start()
        gc_copies.append(copy)
    for copy in gc_copies:
        copy.wait()
    for copy in c_copies + r_copies + z_copies + gz_copies + gr_copies:
        copy.wait_send()


def total_everywhere(part, groups, subs):
    size, width = part.shape
    depth = subs // 2
    rows = size // 2 // groups
    cols = width // depth
    dma = pltpu.SemaphoreType.DMA
    return pl.pallas_call(
        functools.partial(total_kernel, groups, depth),
        out_shape=jax.ShapeDtypeStruct((size, width), jnp.float32),
        in_specs=[pl.BlockSpec(memory_space=pltpu.VMEM)],
        out_specs=pl.BlockSpec(memory_space=pltpu.VMEM),
        scratch_shapes=[
            pltpu.VMEM((groups, rows, width), jnp.float32),
            pltpu.VMEM((groups, rows, width), jnp.float32),
            pltpu.VMEM((groups - 1, rows, width), jnp.float32),
            pltpu.VMEM((depth - 1, rows, cols), jnp.float32),
            pltpu.VMEM((depth - 1, rows, cols), jnp.float32),
            dma((groups,)), dma((groups,)),
            dma((groups - 1,)), dma((groups - 1,)),
            dma((depth - 1,)), dma((depth - 1,)),
            dma((depth - 1,)), dma((depth - 1,)),
            dma((depth, groups - 1)), dma((depth, groups - 1)),
            dma((groups,)), dma((groups,)),
        ],
        compiler_params=pltpu.CompilerParams(
            collective_id=1, has_side_effects=True, vmem_limit_bytes=VMEM_LIMIT
        ),
        name="total_everywhere",
    )(part)


def owner_kernel(groups, subs, part_ref, out_ref, s_in, r_out, r_in, s_send, s_recv, r_send, r_recv):
    r = lax.axis_index("rows")
    s = lax.axis_index("sub")

    def s_peer(step):
        return (r, lax.rem(s + step, subs))

    def r_peer(step):
        return (lax.rem(r + step, groups), s)

    greet(
        [s_peer(step) for step in range(1, subs)] + [r_peer(step) for step in range(1, groups)]
    )
    s_copies = []
    for step in range(1, subs):
        copy = push(part_ref.at[lax.rem(s + step, subs)], s_in.at[step - 1], s_send.at[step - 1], s_recv.at[step - 1], s_peer(step))
        copy.start()
        s_copies.append(copy)
    total = part_ref[s].astype(jnp.float32)
    for step in range(1, subs):
        s_copies[step - 1].wait_recv()
        total = total + s_in[step - 1].astype(jnp.float32)
    r_out[...] = total
    r_copies = []
    for step in range(1, groups):
        copy = push(r_out, r_in.at[step - 1], r_send.at[step - 1], r_recv.at[step - 1], r_peer(step))
        copy.start()
        r_copies.append(copy)
    for step in range(1, groups):
        r_copies[step - 1].wait_recv()
        total = total + r_in[step - 1]
    out_ref[...] = total
    for copy in s_copies + r_copies:
        copy.wait_send()


def total_at_owner(parts, groups):
    subs, width, codewords = parts.shape
    dma = pltpu.SemaphoreType.DMA
    return pl.pallas_call(
        functools.partial(owner_kernel, groups, subs),
        out_shape=jax.ShapeDtypeStruct((width, codewords), jnp.float32),
        in_specs=[pl.BlockSpec(memory_space=pltpu.VMEM)],
        out_specs=pl.BlockSpec(memory_space=pltpu.VMEM),
        scratch_shapes=[
            pltpu.VMEM((subs - 1, width, codewords), parts.dtype),
            pltpu.VMEM((width, codewords), jnp.float32),
            pltpu.VMEM((groups - 1, width, codewords), jnp.float32),
            dma((subs - 1,)), dma((subs - 1,)),
            dma((groups - 1,)), dma((groups - 1,)),
        ],
        compiler_params=pltpu.CompilerParams(
            collective_id=2, has_side_effects=True, vmem_limit_bytes=VMEM_LIMIT
        ),
        name="total_at_owner",
    )(parts)


def one_hot_codes(code_block, count_codes):
    levels = lax.broadcasted_iota(jnp.int32, code_block.shape + (count_codes,), 2)
    return (code_block[:, :, None] == levels).astype(jnp.bfloat16)


def newton_step(whole):
    dot = functools.partial(
        jnp.dot, precision=lax.Precision.HIGH, preferred_element_type=jnp.float32
    )
    gram = lax.dot_general(
        whole, whole, (((1,), (1,)), ((), ())),
        precision=lax.Precision.HIGH, preferred_element_type=jnp.float32,
    )
    mixer = coef_b * gram + coef_c * dot(gram, gram)
    return coef_a * whole + dot(mixer, whole)


def body(groups, subs, embeddings, codes, codebook):
    subspaces, local_rows = codes.shape
    count_codes, own_width = codebook.shape
    width = embeddings.shape[1]
    sub_width = width // subspaces
    me = lax.axis_index("sub")
    one_hot = one_hot_codes(codes, count_codes)
    counts = lax.psum(jnp.sum(one_hot, axis=1, dtype=jnp.float32), ("rows", "sub"))

    table = gather_columns(codebook.T, subs).reshape(subspaces, sub_width, count_codes)
    decoded = jnp.einsum("mnk,mjk->nmj", one_hot, table, preferred_element_type=jnp.float32)
    decoded = decoded.reshape(local_rows, width).astype(jnp.bfloat16)
    partial_cov = lax.dot_general(
        embeddings, decoded, (((0,), (0,)), ((), ())), preferred_element_type=jnp.float32
    )
    cross_cov = total_everywhere(partial_cov, groups, subs)
    frob_scale = jnp.sqrt(jnp.sum(cross_cov * cross_cov)) + frob_eps
    whole = cross_cov / frob_scale
    for unused in range(NS_STEPS):
        whole = newton_step(whole)
    panel_rows = width // subs
    panel = lax.dynamic_slice_in_dim(whole, me * panel_rows, panel_rows, axis=0)
    rotated = jnp.dot(
        embeddings, whole.astype(jnp.bfloat16), preferred_element_type=jnp.float32
    ).astype(jnp.bfloat16)
    part_sums = jnp.einsum(
        "mnk,nmj->mjk", one_hot, rotated.reshape(local_rows, subspaces, sub_width),
        preferred_element_type=jnp.float32,
    )
    part_sums = part_sums.reshape(subs, own_width, count_codes).astype(jnp.bfloat16)
    code_sums = total_at_owner(part_sums, groups).T
    own_subspaces = subspaces // subs
    own_counts = lax.dynamic_slice_in_dim(counts, me * own_subspaces, own_subspaces, axis=0).T
    spread = jnp.repeat(own_counts, sub_width, axis=1)
    new_codebook = (code_sums + codebook.astype(jnp.float32)) / (spread + 1.0)
    return (panel, rotated, new_codebook)


def solution(mesh):
    in_specs = (P(("rows", "sub"), None), P(None, ("rows", "sub")), P(None, "sub"))
    out_specs = (P("sub", None), P(("rows", "sub"), None), P(None, "sub"))
    whole_body = functools.partial(body, mesh.shape["rows"], mesh.shape["sub"])
    return jax.shard_map(
        whole_body, mesh=mesh, in_specs=in_specs, out_specs=out_specs, check_vma=False
    )
```

```python
import functools
import math

import jax
import jax.numpy as jnp
from jax import lax
from jax.experimental import pallas as pl
from jax.experimental.pallas import tpu as pltpu
from jax.sharding import PartitionSpec as P

NS_STEPS = 3


coef_a = 3.4445
coef_b = -4.775
coef_c = 2.0315
frob_eps = 1e-07
MESH = pl.DeviceIdType.MESH
VMEM_LIMIT = 56 * 1024 * 1024


def place():
    sub = lax.axis_index("sub")
    return lax.axis_index("rows"), sub // 2, sub % 2


def greet(peers):
    barrier = pltpu.get_barrier_semaphore()
    for peer in peers:
        pl.semaphore_signal(barrier, inc=1, device_id=peer, device_id_type=MESH)
    pl.semaphore_wait(barrier, len(peers))


def push(src, dst, send_sem, recv_sem, peer):
    return pltpu.make_async_remote_copy(
        src_ref=src,
        dst_ref=dst,
        send_sem=send_sem,
        recv_sem=recv_sem,
        device_id=peer,
        device_id_type=MESH,
    )


def gather_kernel(depth, block_ref, out_ref, z_send, z_recv, c_send, c_recv, local_sem):
    r, z, c = place()
    width = block_ref.shape[0]

    def slot(z_at, c_at):
        return out_ref.at[pl.ds(pl.multiple_of((z_at * 2 + c_at) * width, width), width)]

    def z_peer(step):
        return (r, lax.rem(z + step, depth) * 2 + c)

    partner = (r, z * 2 + 1 - c)
    greet([partner] + [z_peer(step) for step in range(1, depth)])
    z_copies = []
    for step in range(1, depth):
        copy = push(block_ref, slot(z, c), z_send.at[step - 1], z_recv.at[step - 1], z_peer(step))
        copy.start()
        z_copies.append(copy)
    own = pltpu.make_async_copy(block_ref, slot(z, c), local_sem)
    own.start()
    c_copies = [push(block_ref, slot(z, c), c_send.at[0], c_recv.at[0], partner)]
    c_copies[0].start()
    for step in range(1, depth):
        z_copies[step - 1].wait_recv()
        source = lax.rem(z - step + depth, depth)
        copy = push(slot(source, c), slot(source, c), c_send.at[step], c_recv.at[step], partner)
        copy.start()
        c_copies.append(copy)
    for copy in c_copies:
        copy.wait()
    for copy in z_copies:
        copy.wait_send()
    own.wait()


def gather_columns(block, subs):
    width, codewords = block.shape
    depth = subs // 2
    return pl.pallas_call(
        functools.partial(gather_kernel, depth),
        out_shape=jax.ShapeDtypeStruct((width * subs, codewords), block.dtype),
        in_specs=[pl.BlockSpec(memory_space=pltpu.VMEM)],
        out_specs=pl.BlockSpec(memory_space=pltpu.VMEM),
        scratch_shapes=[
            pltpu.SemaphoreType.DMA((max(depth - 1, 1),)),
            pltpu.SemaphoreType.DMA((max(depth - 1, 1),)),
            pltpu.SemaphoreType.DMA((depth,)),
            pltpu.SemaphoreType.DMA((depth,)),
            pltpu.SemaphoreType.DMA,
        ],
        compiler_params=pltpu.CompilerParams(
            collective_id=0, has_side_effects=True, vmem_limit_bytes=VMEM_LIMIT
        ),
        name="gather_columns",
    )(block)


def total_kernel(groups, depth, split, part_ref, out_ref, *scratch):
    (
        a_core, b_core, a_one, a_one_in, b_one, b_one_in, a_two, a_two_in, b_two, b_two_in
    ) = scratch[:10]
    sems = scratch[10:]
    ac, bc, a1, b1, a2, b2, ag2, bg2, ag1, bg1, agc, bgc = [
        (sems[2 * i], sems[2 * i + 1]) for i in range(12)
    ]
    r, z, c = place()
    size, width = part_ref.shape
    half = size // 2
    a_rows = split // groups
    b_all = half - split
    b_rows = b_all // groups
    cols = width // depth
    partner = (r, z * 2 + 1 - c)
    copies = []

    def r_peer(step):
        return (lax.rem(r + step, groups), z * 2 + c)

    def z_peer(step):
        return (r, lax.rem(z + step, depth) * 2 + c)

    def a_chunk(core_at, row_at):
        return pl.ds(pl.multiple_of(core_at * half + row_at * a_rows, 8), a_rows)

    def b_whole(core_at):
        return pl.ds(pl.multiple_of(core_at * half + split, 8), b_all)

    def b_chunk(core_at, row_at):
        return pl.ds(pl.multiple_of(core_at * half + split + row_at * b_rows, 8), b_rows)

    def band(z_at):
        return pl.ds(pl.multiple_of(z_at * cols, cols), cols)

    def send(src, dst, sem, at, peer):
        copy = push(src, dst, sem[0].at[at], sem[1].at[at], peer)
        copy.start()
        copies.append(copy)
        return copy

    def share(spot, sem, at, peer):
        return send(out_ref.at[spot], out_ref.at[spot], sem, at, peer)

    greet(
        [partner]
        + [r_peer(step) for step in range(1, groups)]
        + [z_peer(step) for step in range(1, depth)]
    )
    a_order = list(range(1, groups)) + [0]
    b_order = list(range(1, depth)) + [0]
    rounds = max(groups, depth)
    a_in, b_in = [], []
    for at in range(rounds):
        if at < groups:
            q = lax.rem(r + a_order[at], groups)
            a_in.append(send(part_ref.at[a_chunk(1 - c, q)], a_core.at[at], ac, at, partner))
        if at < depth:
            q = lax.rem(z + b_order[at], depth)
            b_in.append(send(part_ref.at[b_whole(1 - c), band(q)], b_core.at[at], bc, at, partner))
    a_next, b_next = [], []
    for at in range(rounds):
        if at < groups:
            step = a_order[at]
            a_in[at].wait_recv()
            a_one[at] = part_ref[a_chunk(c, lax.rem(r + step, groups))] + a_core[at]
            if step > 0:
                a_next.append(send(a_one.at[at], a_one_in.at[at], a1, at, r_peer(step)))
        if at < depth:
            step = b_order[at]
            b_in[at].wait_recv()
            b_one[at] = part_ref[b_whole(c), band(lax.rem(z + step, depth))] + b_core[at]
            if step > 0:
                b_next.append(send(b_one.at[at], b_one_in.at[at], b1, at, z_peer(step)))

    def b_sum(row_at):
        spot = pl.ds(pl.multiple_of(row_at * b_rows, 8), b_rows)
        total = b_one[depth - 1, spot]
        for at in range(depth - 1):
            total = total + b_one_in[at, spot]
        return total

    def a_sum(z_at):
        total = a_one[groups - 1, :, band(z_at)]
        for at in range(groups - 1):
            total = total + a_one_in[at, :, band(z_at)]
        return total

    for copy in b_next:
        copy.wait_recv()
    b_last = []
    for step in range(1, groups):
        b_two[step - 1] = b_sum(lax.rem(r + step, groups))
        b_last.append(send(b_two.at[step - 1], b_two_in.at[step - 1], b2, step - 1, r_peer(step)))
    for copy in a_next:
        copy.wait_recv()
    a_last = []
    for step in range(1, depth):
        a_two[step - 1] = a_sum(lax.rem(z + step, depth))
        a_last.append(send(a_two.at[step - 1], a_two_in.at[step - 1], a2, step - 1, z_peer(step)))

    total = b_sum(r)
    for step in range(1, groups):
        b_last[step - 1].wait_recv()
        total = total + b_two_in[step - 1]
    b_own = (b_chunk(c, r), band(z))
    out_ref[b_own] = total
    b_near = [share(b_own, bg2, step - 1, r_peer(step)) for step in range(1, groups)]
    total = a_sum(z)
    for step in range(1, depth):
        a_last[step - 1].wait_recv()
        total = total + a_two_in[step - 1]
    a_own = (a_chunk(c, r), band(z))
    out_ref[a_own] = total
    a_near = [share(a_own, ag2, step - 1, z_peer(step)) for step in range(1, depth)]

    for copy in b_near:
        copy.wait_recv()
    b_band = (b_whole(c), band(z))
    b_far = [share(b_band, bg1, step - 1, z_peer(step)) for step in range(1, depth)]
    a_far = []
    for at in range(depth):
        if at > 0:
            a_near[at - 1].wait_recv()
        block = (a_chunk(c, r), band(lax.rem(z - at + depth, depth)))
        a_far.append([share(block, ag1, at * (groups - 1) + step - 1, r_peer(step)) for step in range(1, groups)])
    ends = []
    for at in range(rounds):
        if at < depth:
            if at > 0:
                b_far[at - 1].wait_recv()
            block = (b_whole(c), band(lax.rem(z - at + depth, depth)))
            ends.append(share(block, bgc, at, partner))
        if at < groups:
            if at > 0:
                for arrived in a_far:
                    arrived[at - 1].wait_recv()
            block = (a_chunk(c, lax.rem(r - at + groups, groups)), slice(None))
            ends.append(share(block, agc, at, partner))
    for copy in ends:
        copy.wait_recv()
    for copy in copies:
        copy.wait_send()


def total_everywhere(part, groups, subs):
    size, width = part.shape
    depth = subs // 2
    half = size // 2
    unit = 8 * groups
    split = max(half * 3 // 4 // unit, 1) * unit
    rest = half - split
    cols = width // depth
    f32 = functools.partial(pltpu.VMEM, dtype=jnp.float32)
    dma = pltpu.SemaphoreType.DMA
    pairs = [
        groups, depth, groups - 1, depth - 1, depth - 1, groups - 1,
        depth - 1, groups - 1, depth * (groups - 1), depth - 1, groups, depth,
    ]
    return pl.pallas_call(
        functools.partial(total_kernel, groups, depth, split),
        out_shape=jax.ShapeDtypeStruct((size, width), jnp.float32),
        in_specs=[pl.BlockSpec(memory_space=pltpu.VMEM)],
        out_specs=pl.BlockSpec(memory_space=pltpu.VMEM),
        scratch_shapes=[
            f32((groups, split // groups, width)),
            f32((depth, rest, cols)),
            f32((groups, split // groups, width)),
            f32((groups - 1, split // groups, width)),
            f32((depth, rest, cols)),
            f32((depth - 1, rest, cols)),
            f32((depth - 1, split // groups, cols)),
            f32((depth - 1, split // groups, cols)),
            f32((groups - 1, rest // groups, cols)),
            f32((groups - 1, rest // groups, cols)),
        ]
        + [dma((count,)) for count in pairs for unused in range(2)],
        compiler_params=pltpu.CompilerParams(
            collective_id=1, has_side_effects=True, vmem_limit_bytes=VMEM_LIMIT
        ),
        name="total_everywhere",
    )(part)


def owner_kernel(
    groups, depth, part_ref, out_ref, c_in, z_out, z_in, r_out, r_in,
    c_send, c_recv, z_send, z_recv, r_send, r_recv,
):
    r, z, c = place()
    partner = (r, z * 2 + 1 - c)

    def z_peer(step):
        return (r, lax.rem(z + step, depth) * 2 + c)

    def r_peer(step):
        return (lax.rem(r + step, groups), z * 2 + c)

    greet(
        [partner]
        + [z_peer(step) for step in range(1, depth)]
        + [r_peer(step) for step in range(1, groups)]
    )
    order = list(range(1, depth)) + [0]
    c_copies = []
    for at, step in enumerate(order):
        block = lax.rem(z + step, depth) * 2
        copy = push(part_ref.at[block + 1 - c], c_in.at[at], c_send.at[at], c_recv.at[at], partner)
        copy.start()
        c_copies.append(copy)
    z_copies = []
    for at, step in enumerate(order):
        c_copies[at].wait_recv()
        block = lax.rem(z + step, depth) * 2 + c
        total = part_ref[block].astype(jnp.float32) + c_in[at].astype(jnp.float32)
        if step > 0:
            z_out[at] = total.astype(z_out.dtype)
            copy = push(z_out.at[at], z_in.at[at], z_send.at[at], z_recv.at[at], z_peer(step))
            copy.start()
            z_copies.append(copy)
    for at in range(depth - 1):
        z_copies[at].wait_recv()
        total = total + z_in[at].astype(jnp.float32)
    r_out[...] = total.astype(r_out.dtype)
    r_copies = []
    for step in range(1, groups):
        copy = push(r_out, r_in.at[step - 1], r_send.at[step - 1], r_recv.at[step - 1], r_peer(step))
        copy.start()
        r_copies.append(copy)
    total = r_out[...].astype(jnp.float32)
    for step in range(1, groups):
        r_copies[step - 1].wait_recv()
        total = total + r_in[step - 1].astype(jnp.float32)
    out_ref[...] = total
    for copy in c_copies + z_copies + r_copies:
        copy.wait_send()


def total_at_owner(parts, groups):
    subs, width, codewords = parts.shape
    depth = subs // 2
    dma = pltpu.SemaphoreType.DMA
    return pl.pallas_call(
        functools.partial(owner_kernel, groups, depth),
        out_shape=jax.ShapeDtypeStruct((width, codewords), jnp.float32),
        in_specs=[pl.BlockSpec(memory_space=pltpu.VMEM)],
        out_specs=pl.BlockSpec(memory_space=pltpu.VMEM),
        scratch_shapes=[
            pltpu.VMEM((depth, width, codewords), parts.dtype),
            pltpu.VMEM((depth - 1, width, codewords), parts.dtype),
            pltpu.VMEM((depth - 1, width, codewords), parts.dtype),
            pltpu.VMEM((width, codewords), parts.dtype),
            pltpu.VMEM((groups - 1, width, codewords), parts.dtype),
            dma((depth,)), dma((depth,)),
            dma((depth - 1,)), dma((depth - 1,)),
            dma((groups - 1,)), dma((groups - 1,)),
        ],
        compiler_params=pltpu.CompilerParams(
            collective_id=2, has_side_effects=True, vmem_limit_bytes=VMEM_LIMIT
        ),
        name="total_at_owner",
    )(parts)


def one_hot_codes(code_block, count_codes):
    levels = lax.broadcasted_iota(jnp.int32, code_block.shape + (count_codes,), 2)
    return (code_block[:, :, None] == levels).astype(jnp.bfloat16)


def newton_step(whole, inverse=None):
    fine = lax.Precision.HIGH
    inner = fine if inverse is None else lax.Precision.DEFAULT
    gram = lax.dot_general(
        whole, whole, (((1,), (1,)), ((), ())),
        precision=inner, preferred_element_type=jnp.float32,
    )
    if inverse is not None:
        gram = gram * (inverse * inverse)
    square = jnp.dot(gram, gram, precision=inner, preferred_element_type=jnp.float32)
    mixer = coef_b * gram + coef_c * square
    stepped = coef_a * whole + jnp.dot(
        mixer, whole, precision=fine, preferred_element_type=jnp.float32
    )
    return stepped if inverse is None else stepped * inverse


def body(groups, subs, embeddings, codes, codebook):
    subspaces, local_rows = codes.shape
    count_codes, own_width = codebook.shape
    width = embeddings.shape[1]
    sub_width = width // subspaces
    me = lax.axis_index("sub")
    one_hot = one_hot_codes(codes, count_codes)
    counts = lax.psum(jnp.sum(one_hot, axis=1, dtype=jnp.float32), ("rows", "sub"))

    table = gather_columns(codebook.T, subs).reshape(subspaces, sub_width, count_codes)
    decoded = jnp.einsum("mnk,mjk->nmj", one_hot, table, preferred_element_type=jnp.float32)
    decoded = decoded.reshape(local_rows, width).astype(jnp.bfloat16)
    partial_cov = lax.dot_general(
        embeddings, decoded, (((0,), (0,)), ((), ())), preferred_element_type=jnp.float32
    )
    cross_cov = total_everywhere(partial_cov, groups, subs)
    frob_scale = jnp.sqrt(jnp.sum(cross_cov * cross_cov)) + frob_eps
    whole = newton_step(cross_cov, 1.0 / frob_scale)
    for unused in range(NS_STEPS - 1):
        whole = newton_step(whole)
    panel_rows = width // subs
    panel = lax.dynamic_slice_in_dim(whole, me * panel_rows, panel_rows, axis=0)
    rotated = jnp.dot(
        embeddings, whole.astype(jnp.bfloat16), preferred_element_type=jnp.float32
    ).astype(jnp.bfloat16)
    part_sums = jnp.einsum(
        "mnk,nmj->mjk", one_hot, rotated.reshape(local_rows, subspaces, sub_width),
        preferred_element_type=jnp.float32,
    )
    part_sums = part_sums.reshape(subs, own_width, count_codes).astype(jnp.bfloat16)
    code_sums = total_at_owner(part_sums, groups).T
    own_subspaces = subspaces // subs
    own_counts = lax.dynamic_slice_in_dim(counts, me * own_subspaces, own_subspaces, axis=0).T
    spread = jnp.repeat(own_counts, sub_width, axis=1)
    new_codebook = (code_sums + codebook.astype(jnp.float32)) / (spread + 1.0)
    return (panel, rotated, new_codebook)


def solution(mesh):
    in_specs = (P(("rows", "sub"), None), P(None, ("rows", "sub")), P(None, "sub"))
    out_specs = (P("sub", None), P(("rows", "sub"), None), P(None, "sub"))
    whole_body = functools.partial(body, mesh.shape["rows"], mesh.shape["sub"])
    return jax.shard_map(
        whole_body, mesh=mesh, in_specs=in_specs, out_specs=out_specs, check_vma=False
    )
```
